256 devices in a mesh: section: 32 (over y_hi, z, core), ctx: 8 (over y_lo, x).
Axes of the slice: x: 4, y: 4 (y_hi: 2, y_lo: 2; y = y_hi * 2 + y_lo), z: 8, core: 2. Of those that a mesh axis runs over, the one named last changes fastest.
Arguments:
- queries: bfloat16 [32, 1024, 8192], P('section', 'ctx'), may hold values from -6 to 6
- key_states: bfloat16 [32, 1024, 1024], P('section', 'ctx'), may hold values from -6 to 6
- value_states: bfloat16 [32, 1024, 1024], P('section', 'ctx'), may hold values from -1.5 to 1.5
- out_grad: bfloat16 [32, 1024, 8192], P('section', 'ctx'), may hold values from -6 to 6
- node_end: int32 [32, 1024], P('section'), may hold values from 1 to 1024, as said below
- block_list: int32 [32, 8, 8], P('section'), may hold values from 0 to 7, as said below
- block_count: int32 [32, 8], P('section'), may hold values from 1 to 8, as said below
Outputs:
- query_grads: bfloat16 [32, 1024, 8192], P('section', 'ctx')
- key_grads: bfloat16 [32, 1024, 1024], P('section', 'ctx')
- value_grads: bfloat16 [32, 1024, 1024], P('section', 'ctx')
The draws below stay inside these ranges and needn't reach their ends.
Inputs may be any that keep to these rules, and one draw needn't show every extreme that they name: Each section packs search trees one after another, each in preorder; node_end[s, j] is one past the last node of node j's subtree, so j is an ancestor of i (or i itself) exactly when j <= i < node_end[s, j]. Row b of block_list[s] lists, in increasing order, every key block that holds an ancestor (or the node itself) of some node of query block b, and no other; b itself is always listed; entries after the first block_count[s, b] are 0. block_count[s, b] is the number of listed key blocks of query block b, at most b + 1.
All inputs are finite; a program needn't handle non-finite values.
Results may differ from the reference program's by a relative error of at most 0.0053.
Values may be sent and summed in bfloat16 or wider, within the bound.
No kernel may reach another device: no remote copies, remote signals or barrier semaphores. Data moves between devices by JAX's collectives and lax.ppermute only.
A program may use at most 128 MiB of HBM per device.

```python
import math
import jax
import jax.numpy as jnp
from jax import lax

HEADS = 64
KV_HEADS = 8
HEAD_DIM = 128
BLK = 128
SECTIONS = 32
SEQ = 1024
NBLK = 8


def tree_depths(key):
    base = jax.random.fold_in(key, 11)

    def one_section(section_index):
        section_key = jax.random.fold_in(base, section_index)
        first_key, second_key, third_key = jax.random.split(section_key, 3)
        fresh = jax.random.randint(first_key, (SEQ,), 0, 2048)
        deeper = jax.random.randint(second_key, (SEQ,), 0, 4)
        jumps = jax.random.randint(third_key, (SEQ,), 0, 1048576)
        position = jnp.arange(SEQ, dtype=jnp.int32)
        forced = section_index == 0

        def advance(carry, inputs):
            depth, floor_depth = carry
            fresh_now, deeper_now, jump_now, place = inputs
            marker = forced & (place > 0) & (place % BLK == 0)
            rooted = (place == 0) | (fresh_now == 0) & jnp.logical_not(forced)
            climbs = (deeper_now < 3) | (depth == 0) | marker
            lowered = floor_depth + 1 + jump_now % jnp.maximum(depth - floor_depth, 1)
            following = jnp.where(rooted, 0, jnp.where(climbs, depth + 1, lowered)).astype(jnp.int32)
            next_floor = jnp.where(marker, following, floor_depth).astype(jnp.int32)
            return ((following, next_floor), following)
        unused, depth = lax.scan(advance, (jnp.int32(0), jnp.int32(0)), (fresh, deeper, jumps, position))
        return depth
    return lax.map(one_section, jnp.arange(SECTIONS, dtype=jnp.int32))


def tree_tables(key):
    depth = tree_depths(key)
    position = jnp.arange(SEQ, dtype=jnp.int32)
    blocks = jnp.arange(NBLK, dtype=jnp.int32)

    def one_section(depth_row):
        later = (position[None, :] > position[:, None]) & (depth_row[None, :] <= depth_row[:, None])
        subtree_end = jnp.min(jnp.where(later, position[None, :], SEQ), axis=1).astype(jnp.int32)
        ancestry = (position[None, :] <= position[:, None]) & (position[:, None] < subtree_end[None, :])
        block_flags = jnp.any(ancestry.reshape(NBLK, BLK, NBLK, BLK), axis=(1, 3))
        ranked = jnp.argsort(jnp.where(block_flags, blocks[None, :], NBLK + blocks[None, :]), axis=1).astype(jnp.int32)
        counts = jnp.sum(block_flags.astype(jnp.int32), axis=1).astype(jnp.int32)
        block_rows = jnp.where(blocks[None, :] < counts[:, None], ranked, 0).astype(jnp.int32)
        return (subtree_end, block_rows, counts)
    return lax.map(one_section, depth)


def draw_node_end(key, part):
    return tree_tables(key)[0]


def draw_block_list(key, part):
    return tree_tables(key)[1]


def draw_block_count(key, part):
    return tree_tables(key)[2]


def draw_queries(key, part):
    shape = (SECTIONS, SEQ, KV_HEADS, HEADS // KV_HEADS, HEAD_DIM)
    base = jnp.clip(jax.random.normal(jax.random.fold_in(key, 22), shape, jnp.float32), -6.0, 6.0)
    return base.reshape(SECTIONS, SEQ, HEADS * HEAD_DIM).astype(jnp.bfloat16)


def draw_key_states(key, part):
    shape = (SECTIONS, SEQ, KV_HEADS, HEAD_DIM)
    base = jnp.clip(jax.random.normal(jax.random.fold_in(key, 23), shape, jnp.float32), -6.0, 6.0)
    return base.reshape(SECTIONS, SEQ, KV_HEADS * HEAD_DIM).astype(jnp.bfloat16)


def block_scale(stream_key, dims, pieces, least, largest):
    def one(axis_at, parts):
        draws = jax.random.uniform(jax.random.fold_in(jax.random.fold_in(stream_key, 6), axis_at), (parts,), jnp.float32, least / len(pieces), largest / len(pieces))
        return jnp.repeat(jnp.exp(draws), dims[axis_at] // parts).reshape((-1,) + (1,) * (len(dims) - axis_at - 1))

    loudness = one(*pieces[0])
    for cut in pieces[1:]:
        loudness = loudness * one(*cut)
    return loudness


def centred(key, shape, scale, bound, cuts=(), kind=jnp.bfloat16):
    result = jax.random.normal(key, shape, jnp.float32) * scale
    if len(cuts) > 0:
        result = block_scale(key, shape, cuts, -0.22, 0.18) * result
    return jnp.clip(result, min=-bound, max=bound).astype(kind)


def setup_inputs(seed: int = 0) -> dict:
    key_of = jax.random.split(jax.random.key(seed), 8)
    return {
        "queries": draw_queries(jax.random.fold_in(key_of[7], 71), 0),
        "key_states": draw_key_states(jax.random.fold_in(key_of[7], 71), 0),
        "value_states": centred(key_of[2], (SECTIONS, SEQ, KV_HEADS * HEAD_DIM), 0.25, 1.5, ((0, 32), (1, 8))),
        "out_grad": centred(key_of[3], (SECTIONS, SEQ, HEADS * HEAD_DIM), 1.0, 6.0, ((0, 32), (1, 8))),
        "node_end": draw_node_end(jax.random.fold_in(key_of[7], 71), 0),
        "block_list": draw_block_list(jax.random.fold_in(key_of[7], 71), 0),
        "block_count": draw_block_count(jax.random.fold_in(key_of[7], 71), 0),
    }


def allowed_mask(end_row, list_rows, count_row):
    position = jnp.arange(SEQ, dtype=jnp.int32)
    ancestry = (position[None, :] <= position[:, None]) & (position[:, None] < end_row[None, :])
    entries = jnp.arange(NBLK, dtype=jnp.int32)
    listed = jnp.any((list_rows[:, :, None] == entries[None, None, :]) & (entries[None, :, None] < count_row[:, None, None]), axis=1)
    spread = jnp.repeat(jnp.repeat(listed, BLK, axis=0), BLK, axis=1)
    return ancestry & spread

def group_grads(query_rows, grad_rows, key_rows, value_rows, allowed):
    row_total = query_rows.shape[0]
    scale = 1.0 / math.sqrt(HEAD_DIM)
    query_heads = query_rows.reshape(row_total, -1, HEAD_DIM).astype(jnp.float32)
    grad_heads = grad_rows.reshape(row_total, -1, HEAD_DIM).astype(jnp.float32)
    key_float = key_rows.astype(jnp.float32)
    value_float = value_rows.astype(jnp.float32)
    scores = jnp.einsum('qhd,kd->hqk', query_heads, key_float) * scale
    scores = jnp.where(allowed[None], scores, -jnp.inf)
    row_max = lax.optimization_barrier(jnp.max(scores, axis=2, keepdims=True))
    exponent = jnp.exp(scores - row_max)
    attention = exponent / lax.optimization_barrier(jnp.sum(exponent, axis=2, keepdims=True))
    attention_half = attention.astype(jnp.bfloat16)
    weight_grad = jnp.einsum('qhd,kd->hqk', grad_heads, value_float)
    row_delta = lax.optimization_barrier(jnp.sum(attention * weight_grad, axis=2, keepdims=True))
    score_grad = (attention * (weight_grad - row_delta) * scale).astype(jnp.bfloat16)
    score_float = score_grad.astype(jnp.float32)
    query_grad = jnp.einsum('hqk,kd->qhd', score_float, key_float).reshape(row_total, -1)
    key_grad = jnp.einsum('hqk,qhd->kd', score_float, query_heads)
    value_grad = jnp.einsum('hqk,qhd->kd', attention_half.astype(jnp.float32), grad_heads)
    return (query_grad, key_grad, value_grad)

def section_grads(section_inputs):
    query_all, key_all, value_all, grad_all, end_row, list_rows, count_row = section_inputs
    allowed = allowed_mask(end_row, list_rows, count_row)
    width = HEADS // KV_HEADS * HEAD_DIM
    query_parts = []
    key_parts = []
    value_parts = []
    for group_index in range(KV_HEADS):
        query_grad, key_grad, value_grad = group_grads(query_all[:, group_index * width:(group_index + 1) * width], grad_all[:, group_index * width:(group_index + 1) * width], key_all[:, group_index * HEAD_DIM:(group_index + 1) * HEAD_DIM], value_all[:, group_index * HEAD_DIM:(group_index + 1) * HEAD_DIM], allowed)
        query_parts.append(query_grad)
        key_parts.append(key_grad)
        value_parts.append(value_grad)
    return (jnp.concatenate(query_parts, axis=1).astype(jnp.bfloat16), jnp.concatenate(key_parts, axis=1).astype(jnp.bfloat16), jnp.concatenate(value_parts, axis=1).astype(jnp.bfloat16))

def reference(queries, key_states, value_states, out_grad, node_end, block_list, block_count):
    query_grad, key_grad, value_grad = lax.map(section_grads, (queries, key_states, value_states, out_grad, node_end, block_list, block_count))
    return (jnp.roll(query_grad, -1, axis=0), jnp.roll(key_grad, -1, axis=0), jnp.roll(value_grad, -1, axis=0))
```

```python
import functools
import math

import jax
import jax.numpy as jnp
from jax import lax
from jax.experimental import pallas as pl
from jax.experimental.pallas import tpu as pltpu
from jax.sharding import PartitionSpec as P

HEADS = 64
KV_HEADS = 8
HEAD_DIM = 128
BLK = 128
NBLK = 8
RATIO = HEADS // KV_HEADS
LANES = RATIO * BLK
HALF = 2 * BLK
RING = 4
CHUNKS = 2
GROUPS = KV_HEADS // CHUNKS
SCALE = 1.0 / math.sqrt(HEAD_DIM)
LOG2E = math.log2(math.e)
LOWEST = -3.0e38


def ctx_route(move):
    route = []
    for place in range(NBLK):
        target = move(place // RING, place % RING)
        if target is not None:
            route.append((place, target[0] * RING + target[1] % RING))
    return route


def right(y, x):
    return (y, x + 1)


def left(y, x):
    return (y, x - 1)


def across(y, x):
    return (y, x + 2)


def up(y, x):
    return (1, x) if y == 0 else None


def down(y, x):
    return (0, x) if y == 1 else None


def stay(y, x):
    return (y, x)


def send(block, move):
    return lax.ppermute(block, "ctx", ctx_route(move))


def send_behind(block, move):
    sections = lax.axis_size("section")
    route = []
    for section in range(sections):
        for source, target in ctx_route(move):
            route.append((section * NBLK + source, ((section - 1) % sections) * NBLK + target))
    return lax.ppermute(block, ("section", "ctx"), route)


def nt_dot(a, b):
    return lax.dot_general(a, b, (((1,), (1,)), ((), ())), preferred_element_type=jnp.float32)


def grads_kernel(info, ends_ref, q_ref, g_ref, own_ref, left_ref, right_ref, y_ref, x2_ref, ylr_ref,
                 dq_ref, near_ref, far_ref, side_ref,
                 keys, values, bias, weights, wgrads, tops, dq_acc, pair_acc):
    count = info[0]
    row_place = info[9]
    y = row_place // RING
    x = lax.rem(row_place, RING)
    other = 1 - y
    pairs = lax.div(count + 1, 2)

    def place_of(row, column):
        return row * RING + lax.rem(column + RING, RING)

    @pl.when(pl.program_id(0) == 0)
    def _():
        row = row_place * BLK + lax.broadcasted_iota(jnp.int32, (BLK, BLK), 1)
        inner = lax.broadcasted_iota(jnp.int32, (BLK, BLK), 0)
        for entry in range(NBLK):
            block = info[1 + entry]
            column = block * BLK + inner
            ends = ends_ref[pl.ds(pl.multiple_of(block * BLK, BLK), BLK), :]
            good = (column <= row) & (row < ends) & (entry < count)
            bias[pl.ds(entry * BLK, BLK), :] = jnp.where(good, 0.0, -jnp.inf)

    slots = (
        (own_ref, (), place_of(y, x)),
        (left_ref, (), place_of(y, x - 1)),
        (right_ref, (), place_of(y, x + 1)),
        (y_ref, (), place_of(other, x)),
        (x2_ref, (0,), place_of(y, x + 2)),
        (x2_ref, (1,), place_of(other, x + 2)),
        (ylr_ref, (0,), place_of(other, x - 1)),
        (ylr_ref, (1,), place_of(other, x + 1)),
    )
    for ref, lead, place in slots:
        rows = pl.ds(pl.multiple_of(place * BLK, BLK), BLK)
        keys[rows, :] = ref[(*lead, 0)]
        values[rows, :] = ref[(*lead, 1)]

    pair_acc[...] = jnp.zeros_like(pair_acc)
    dq_acc[...] = jnp.zeros_like(dq_acc)

    def block_rows(entry):
        return pl.ds(pl.multiple_of(info[1 + entry] * BLK, BLK), BLK)

    def both(ref, pair):
        return jnp.concatenate([ref[block_rows(2 * pair), :], ref[block_rows(2 * pair + 1), :]], axis=0)

    def two_heads(ref, part):
        first = part * HALF
        return jnp.concatenate([ref[0, :, first:first + BLK], ref[0, :, first + BLK:first + HALF]], axis=0)

    def first_pass(pair, carry):
        top, total, delta = carry
        key_pair = both(keys, pair)
        value_pair = both(values, pair)
        rows = pl.ds(pl.multiple_of(pair * HALF, HALF), HALF)
        mask = bias[rows, :]
        mask2 = jnp.concatenate([mask, mask], axis=1)
        new_top, new_total, new_delta = [], [], []
        for part in range(RATIO // 2):
            lanes = slice(part * HALF, (part + 1) * HALF)
            scores = nt_dot(key_pair, two_heads(q_ref, part)) + mask2
            wgrad = nt_dot(value_pair, two_heads(g_ref, part))
            old = top[:, lanes]
            now = jnp.maximum(old, jnp.max(scores, axis=0, keepdims=True))
            weight = jnp.exp2((scores - now) * (SCALE * LOG2E))
            shrink = jnp.exp2((old - now) * (SCALE * LOG2E))
            weights[rows, lanes] = weight
            wgrads[rows, lanes] = wgrad
            new_top.append(now)
            new_total.append(total[:, lanes] * shrink + jnp.sum(weight, axis=0, keepdims=True))
            new_delta.append(delta[:, lanes] * shrink + jnp.sum(weight * wgrad, axis=0, keepdims=True))
        top = jnp.concatenate(new_top, axis=1)
        tops[pl.ds(pair, 1), :] = top
        return (top, jnp.concatenate(new_total, axis=1), jnp.concatenate(new_delta, axis=1))

    zero = jnp.zeros((1, LANES), jnp.float32)
    top, total, delta = lax.fori_loop(0, pairs, first_pass, (jnp.full((1, LANES), LOWEST, jnp.float32), zero, zero))
    inverse = 1.0 / total
    delta = delta * inverse

    def second_pass(pair, carry):
        key_pair_t = both(keys, pair).T
        rows = pl.ds(pl.multiple_of(pair * HALF, HALF), HALF)
        factor = jnp.exp2((tops[pl.ds(pair, 1), :] - top) * (SCALE * LOG2E)) * inverse
        key_sum = jnp.zeros((HALF, HEAD_DIM), jnp.float32)
        value_sum = jnp.zeros((HALF, HEAD_DIM), jnp.float32)
        for part in range(RATIO // 2):
            lanes = slice(part * HALF, (part + 1) * HALF)
            attention = weights[rows, lanes] * factor[:, lanes]
            score_grad = (attention * ((wgrads[rows, lanes] - delta[:, lanes]) * SCALE)).astype(jnp.bfloat16)
            value_sum += jnp.dot(attention.astype(jnp.bfloat16), two_heads(g_ref, part), preferred_element_type=jnp.float32)
            key_sum += jnp.dot(score_grad, two_heads(q_ref, part), preferred_element_type=jnp.float32)
            dq_acc[:, lanes] += jnp.dot(key_pair_t, score_grad, preferred_element_type=jnp.float32)

        pair_acc[0, block_rows(2 * pair), :] = key_sum[:BLK]
        pair_acc[1, block_rows(2 * pair), :] = value_sum[:BLK]

        @pl.when(2 * pair + 1 < count)
        def _():
            pair_acc[0, block_rows(2 * pair + 1), :] = key_sum[BLK:]
            pair_acc[1, block_rows(2 * pair + 1), :] = value_sum[BLK:]

        return carry

    lax.fori_loop(0, pairs, second_pass, 0)
    for head in range(RATIO):
        lanes = slice(head * BLK, (head + 1) * BLK)
        dq_ref[:, lanes] = dq_acc[:, lanes].T.astype(jnp.bfloat16)
    outs = (
        (near_ref, (0,), slots[0][2]),
        (near_ref, (1,), slots[1][2]),
        (near_ref, (2,), slots[2][2]),
        (near_ref, (3,), slots[3][2]),
        (far_ref, (0,), slots[4][2]),
        (far_ref, (1,), slots[5][2]),
        (side_ref, (0,), slots[6][2]),
        (side_ref, (1,), slots[7][2]),
    )
    for ref, lead, place in outs:
        rows = pl.ds(pl.multiple_of(place * BLK, BLK), BLK)
        for which in range(2):
            ref[(*lead, which)] = pair_acc[which, rows, :].astype(ref.dtype)


def chunk_grads(chunk, info, ends, queries, out_grad, own, from_left, from_right, from_y, from_x2, from_ylr):
    width = LANES
    wide = pl.BlockSpec((1, BLK, width), lambda g, *_: (0, 0, chunk * GROUPS + g))
    one = pl.BlockSpec((2, BLK, HEAD_DIM), lambda g, *_: (0, 0, g))
    two = pl.BlockSpec((2, 2, BLK, HEAD_DIM), lambda g, *_: (0, 0, 0, g))
    four = pl.BlockSpec((4, 2, BLK, HEAD_DIM), lambda g, *_: (0, 0, 0, g))
    columns = GROUPS * HEAD_DIM
    return pl.pallas_call(
        grads_kernel,
        grid_spec=pltpu.PrefetchScalarGridSpec(
            num_scalar_prefetch=1,
            grid=(GROUPS,),
            in_specs=[pl.BlockSpec((NBLK * BLK, 1), lambda g, *_: (0, 0)), wide, wide, one, one, one, one, two, two],
            out_specs=[pl.BlockSpec((BLK, width), lambda g, *_: (0, g)), four, two, two],
            scratch_shapes=[
                pltpu.VMEM((NBLK * BLK, HEAD_DIM), jnp.bfloat16),
                pltpu.VMEM((NBLK * BLK, HEAD_DIM), jnp.bfloat16),
                pltpu.VMEM((NBLK * BLK, BLK), jnp.float32),
                pltpu.VMEM((NBLK * BLK, LANES), jnp.float32),
                pltpu.VMEM((NBLK * BLK, LANES), jnp.float32),
                pltpu.VMEM((NBLK, LANES), jnp.float32),
                pltpu.VMEM((HEAD_DIM, LANES), jnp.float32),
                pltpu.VMEM((2, NBLK * BLK, HEAD_DIM), jnp.float32),
            ],
        ),
        out_shape=[
            jax.ShapeDtypeStruct((BLK, GROUPS * width), jnp.bfloat16),
            jax.ShapeDtypeStruct((4, 2, BLK, columns), jnp.bfloat16),
            jax.ShapeDtypeStruct((2, 2, BLK, columns), jnp.bfloat16),
            jax.ShapeDtypeStruct((2, 2, BLK, columns), jnp.bfloat16),
        ],
        compiler_params=pltpu.CompilerParams(vmem_limit_bytes=40 * 1024 * 1024),
        cost_estimate=pl.CostEstimate(
            flops=GROUPS * RATIO * NBLK * 10 * BLK ** 3, bytes_accessed=GROUPS * 6 * BLK * width, transcendentals=0
        ),
    )(info, ends, queries, out_grad, own, from_left, from_right, from_y, from_x2, from_ylr)


def wide_sum(*terms):
    return functools.reduce(jnp.add, [term.astype(jnp.float32) for term in terms]).astype(jnp.bfloat16)


def per_device(queries, key_states, value_states, out_grad, node_end, block_list, block_count):
    place = lax.axis_index("ctx")
    info = jnp.concatenate([block_count[0, place][None], block_list[0, place], place[None].astype(jnp.int32)])
    ends = node_end.reshape(NBLK * BLK, 1)
    columns = GROUPS * HEAD_DIM
    query_parts, pair_parts = [], []
    for chunk in range(CHUNKS):
        span = slice(chunk * columns, (chunk + 1) * columns)
        own = jnp.concatenate([key_states[:, :, span], value_states[:, :, span]])
        from_left = send(own, right)
        from_right = send(own, left)
        from_y = send(own, up)
        from_x2 = send(jnp.stack([own, from_y]), across)
        from_ylr = send(jnp.stack([from_left, from_right]), up)
        dq, near, far, side = chunk_grads(
            chunk, info, ends, queries, out_grad, own, from_left, from_right, from_y, from_x2, from_ylr
        )
        query_parts.append(send_behind(dq, stay))
        side_in = send(side, down)
        far_in = send(far, across)
        terms = [
            send_behind(wide_sum(near[0], far_in[0]), stay),
            send_behind(wide_sum(near[1], side_in[0]), left),
            send_behind(wide_sum(near[2], side_in[1]), right),
            send_behind(wide_sum(near[3], far_in[1]), down),
        ]
        pair_parts.append(wide_sum(*terms))
    return (
        jnp.concatenate(query_parts, axis=1)[None],
        jnp.concatenate([part[0:1] for part in pair_parts], axis=2),
        jnp.concatenate([part[1:2] for part in pair_parts], axis=2),
    )


def solution(mesh):
    placed = (
        P("section", "ctx", None),
        P("section", "ctx", None),
        P("section", "ctx", None),
        P("section", "ctx", None),
        P("section", None),
        P("section", None, None),
        P("section", None),
    )
    return jax.shard_map(
        per_device,
        mesh=mesh,
        in_specs=placed,
        out_specs=(P("section", "ctx", None), P("section", "ctx", None), P("section", "ctx", None)),
        check_vma=False,
    )
```

```python
import functools
import math

import jax
import jax.numpy as jnp
from jax import lax
from jax.experimental import pallas as pl
from jax.experimental.pallas import tpu as pltpu
from jax.sharding import PartitionSpec as P

HEADS = 64
KV_HEADS = 8
HEAD_DIM = 128
BLK = 128
NBLK = 8
RATIO = HEADS // KV_HEADS
LANES = RATIO * BLK
HALF = 2 * BLK
RING = 4
SPLIT = (3, 3, 2)
SCALE = 1.0 / math.sqrt(HEAD_DIM)
LOG2E = math.log2(math.e)
LOWEST = -3.0e38


def ctx_route(move):
    route = []
    for place in range(NBLK):
        target = move(place // RING, place % RING)
        if target is not None:
            route.append((place, target[0] * RING + target[1] % RING))
    return route


def right(y, x):
    return (y, x + 1)


def left(y, x):
    return (y, x - 1)


def across(y, x):
    return (y, x + 2)


def up(y, x):
    return (1, x) if y == 0 else None


def down(y, x):
    return (0, x) if y == 1 else None


def send(block, move):
    return lax.ppermute(block, "ctx", ctx_route(move))


def to_previous_section(block):
    sections = lax.axis_size("section")
    return lax.ppermute(block, "section", [((s + 1) % sections, s) for s in range(sections)])


def nt_dot(a, b):
    return lax.dot_general(a, b, (((1,), (1,)), ((), ())), preferred_element_type=jnp.float32)


def grads_kernel(by_block, info, ends_ref, q_ref, g_ref, own_ref, left_ref, right_ref, y_ref, x2_ref, ylr_ref,
                 dq_ref, *refs):
    part_refs, (keys, values, bias, weights, wgrads, tops, dq_acc, pair_acc) = refs[:-8], refs[-8:]
    count = info[0]
    row_place = info[9]
    y = row_place // RING
    x = lax.rem(row_place, RING)
    other = 1 - y
    pairs = lax.div(count + 1, 2)

    def place_of(row, column):
        return row * RING + lax.rem(column + RING, RING)

    @pl.when(pl.program_id(0) == 0)
    def _():
        row = row_place * BLK + lax.broadcasted_iota(jnp.int32, (BLK, BLK), 1)
        inner = lax.broadcasted_iota(jnp.int32, (BLK, BLK), 0)
        for entry in range(NBLK):
            block = info[1 + entry]
            column = block * BLK + inner
            ends = jnp.broadcast_to(ends_ref[pl.ds(block, 1), :], (BLK, BLK)).T
            good = (column <= row) & (row < ends) & (entry < count)
            bias[pl.ds(entry * BLK, BLK), :] = jnp.where(good, 0.0, -jnp.inf)

    slots = (
        (own_ref, (), place_of(y, x)),
        (left_ref, (), place_of(y, x - 1)),
        (right_ref, (), place_of(y, x + 1)),
        (y_ref, (), place_of(other, x)),
        (x2_ref, (0,), place_of(y, x + 2)),
        (x2_ref, (1,), place_of(other, x + 2)),
        (ylr_ref, (0,), place_of(other, x - 1)),
        (ylr_ref, (1,), place_of(other, x + 1)),
    )
    for ref, lead, place in slots:
        rows = pl.ds(pl.multiple_of(place * BLK, BLK), BLK)
        keys[rows, :] = ref[(*lead, 0)]
        values[rows, :] = ref[(*lead, 1)]

    pair_acc[...] = jnp.zeros_like(pair_acc)
    dq_acc[...] = jnp.zeros_like(dq_acc)

    def block_rows(entry):
        return pl.ds(pl.multiple_of(info[1 + entry] * BLK, BLK), BLK)

    def both(ref, pair):
        return jnp.concatenate([ref[block_rows(2 * pair), :], ref[block_rows(2 * pair + 1), :]], axis=0)

    def two_heads(ref, part):
        first = part * HALF
        return jnp.concatenate([ref[0, :, first:first + BLK], ref[0, :, first + BLK:first + HALF]], axis=0)

    def first_pass(pair, carry):
        top, total, delta = carry
        key_pair = both(keys, pair)
        value_pair = both(values, pair)
        rows = pl.ds(pl.multiple_of(pair * HALF, HALF), HALF)
        mask = bias[rows, :]
        mask2 = jnp.concatenate([mask, mask], axis=1)
        new_top, new_total, new_delta = [], [], []
        for part in range(RATIO // 2):
            lanes = slice(part * HALF, (part + 1) * HALF)
            scores = nt_dot(key_pair, two_heads(q_ref, part)) + mask2
            wgrad = nt_dot(value_pair, two_heads(g_ref, part))
            old = top[:, lanes]
            now = jnp.maximum(old, jnp.max(scores, axis=0, keepdims=True))
            weight = jnp.exp2((scores - now) * (SCALE * LOG2E))
            shrink = jnp.exp2((old - now) * (SCALE * LOG2E))
            weights[rows, lanes] = weight
            wgrads[rows, lanes] = wgrad
            new_top.append(now)
            new_total.append(total[:, lanes] * shrink + jnp.sum(weight, axis=0, keepdims=True))
            new_delta.append(delta[:, lanes] * shrink + jnp.sum(weight * wgrad, axis=0, keepdims=True))
        top = jnp.concatenate(new_top, axis=1)
        tops[pl.ds(pair, 1), :] = top
        return (top, jnp.concatenate(new_total, axis=1), jnp.concatenate(new_delta, axis=1))

    zero = jnp.zeros((1, LANES), jnp.float32)
    top, total, delta = lax.fori_loop(0, pairs, first_pass, (jnp.full((1, LANES), LOWEST, jnp.float32), zero, zero))
    inverse = 1.0 / total
    delta = delta * inverse

    def second_pass(pair, carry):
        key_pair_t = both(keys, pair).T
        rows = pl.ds(pl.multiple_of(pair * HALF, HALF), HALF)
        factor = jnp.exp2((tops[pl.ds(pair, 1), :] - top) * (SCALE * LOG2E)) * inverse
        key_sum = jnp.zeros((HALF, HEAD_DIM), jnp.float32)
        value_sum = jnp.zeros((HALF, HEAD_DIM), jnp.float32)
        for part in range(RATIO // 2):
            lanes = slice(part * HALF, (part + 1) * HALF)
            attention = weights[rows, lanes] * factor[:, lanes]
            score_grad = (attention * ((wgrads[rows, lanes] - delta[:, lanes]) * SCALE)).astype(jnp.bfloat16)
            value_sum += jnp.dot(attention.astype(jnp.bfloat16), two_heads(g_ref, part), preferred_element_type=jnp.float32)
            key_sum += jnp.dot(score_grad, two_heads(q_ref, part), preferred_element_type=jnp.float32)
            dq_acc[:, lanes] += jnp.dot(key_pair_t, score_grad, preferred_element_type=jnp.float32)

        pair_acc[0, block_rows(2 * pair), :] = key_sum[:BLK]
        pair_acc[1, block_rows(2 * pair), :] = value_sum[:BLK]

        @pl.when(2 * pair + 1 < count)
        def _():
            pair_acc[0, block_rows(2 * pair + 1), :] = key_sum[BLK:]
            pair_acc[1, block_rows(2 * pair + 1), :] = value_sum[BLK:]

        return carry

    lax.fori_loop(0, pairs, second_pass, 0)
    for head in range(RATIO):
        lanes = slice(head * BLK, (head + 1) * BLK)
        dq_ref[:, lanes] = dq_acc[:, lanes].T.astype(jnp.bfloat16)
    if by_block:
        outs = [(part_refs[0], (block,), block) for block in range(NBLK)]
    else:
        stay_ref, to_left_ref, to_right_ref, far_ref = part_refs
        leads = [(stay_ref, 0), (to_left_ref, 0), (to_right_ref, 0), (stay_ref, 1)]
        leads += [(far_ref, 0), (far_ref, 1), (to_left_ref, 1), (to_right_ref, 1)]
        outs = [(ref, (at,), slot[2]) for (ref, at), slot in zip(leads, slots)]
    for ref, lead, place in outs:
        rows = pl.ds(pl.multiple_of(place * BLK, BLK), BLK)
        for which in range(2):
            ref[(*lead, which)] = pair_acc[which, rows, :].astype(ref.dtype)


def chunk_grads(by_block, at, base, groups, info, ends, queries, out_grad, own, from_left, from_right, from_y, from_x2, from_ylr):
    width = LANES
    wide = pl.BlockSpec((1, BLK, width), lambda g, *_: (0, 0, base + at + g))
    one = pl.BlockSpec((2, BLK, HEAD_DIM), lambda g, *_: (0, 0, at + g))
    two = pl.BlockSpec((2, 2, BLK, HEAD_DIM), lambda g, *_: (0, 0, 0, at + g))
    outs = (NBLK,) if by_block else (2, 2, 2, 2)
    columns = groups * HEAD_DIM
    return pl.pallas_call(
        functools.partial(grads_kernel, by_block),
        grid_spec=pltpu.PrefetchScalarGridSpec(
            num_scalar_prefetch=1,
            grid=(groups,),
            in_specs=[pl.BlockSpec((NBLK, BLK), lambda g, *_: (0, 0)), wide, wide, one, one, one, one, two, two],
            out_specs=[pl.BlockSpec((BLK, width), lambda g, *_: (0, g))]
            + [pl.BlockSpec((n, 2, BLK, HEAD_DIM), lambda g, *_: (0, 0, 0, g)) for n in outs],
            scratch_shapes=[
                pltpu.VMEM((NBLK * BLK, HEAD_DIM), jnp.bfloat16),
                pltpu.VMEM((NBLK * BLK, HEAD_DIM), jnp.bfloat16),
                pltpu.VMEM((NBLK * BLK, BLK), jnp.float32),
                pltpu.VMEM((NBLK * BLK, LANES), jnp.float32),
                pltpu.VMEM((NBLK * BLK, LANES), jnp.float32),
                pltpu.VMEM((NBLK, LANES), jnp.float32),
                pltpu.VMEM((HEAD_DIM, LANES), jnp.float32),
                pltpu.VMEM((2, NBLK * BLK, HEAD_DIM), jnp.float32),
            ],
        ),
        out_shape=[
            jax.ShapeDtypeStruct((BLK, groups * width), jnp.bfloat16),
        ]
        + [jax.ShapeDtypeStruct((n, 2, BLK, columns), jnp.bfloat16) for n in outs],
        compiler_params=pltpu.CompilerParams(vmem_limit_bytes=40 * 1024 * 1024),
        cost_estimate=pl.CostEstimate(
            flops=groups * RATIO * NBLK * 50 * BLK ** 3, bytes_accessed=groups * 6 * BLK * width, transcendentals=0
        ),
    )(info, ends, queries, out_grad, own, from_left, from_right, from_y, from_x2, from_ylr)


def wide_sum(*terms):
    return functools.reduce(jnp.add, [term.astype(jnp.float32) for term in terms]).astype(jnp.bfloat16)


def after(value, *others):
    return lax.optimization_barrier((value, *others))[0]


def per_device(queries, key_states, value_states, out_grad, node_end, block_list, block_count):
    place = lax.axis_index("ctx")
    info = jnp.concatenate([block_count[0, place][None], block_list[0, place], place[None].astype(jnp.int32)])
    ends = node_end.reshape(NBLK, BLK)
    firsts = [sum(SPLIT[:chunk]) for chunk in range(4)]

    def mine(first, end):
        span = slice(firsts[first] * HEAD_DIM, firsts[end] * HEAD_DIM)
        return jnp.concatenate([key_states[:, :, span], value_states[:, :, span]])

    def near_round(own):
        from_y = send(own, up)
        return send(own, right), send(own, left), from_y

    def far_round(own, near):
        sides = send(jnp.stack([near[0], near[1]]), up)
        return send(jnp.stack([own, near[2]]), across), sides

    def joined(*parts):
        return jnp.concatenate(parts, axis=2)

    def reduce_x(to_left, to_right, far):
        return send(to_left, left), send(to_right, right), send(far, across)

    def run(chunk, held, base, *gathered):
        return chunk_grads(
            False, firsts[chunk] - base, base, SPLIT[chunk], held, ends, queries, out_grad, *gathered
        )

    own0 = mine(0, 1)
    near_round0 = near_round(own0)
    far_round0 = far_round(own0, near_round0)
    own12 = mine(1, 3)
    near_round12 = near_round(own12)
    far_round12 = far_round(own12, near_round12)
    gathered12 = (own12, *near_round12, *far_round12)

    dq0, stay0, *away0 = run(0, after(info, *near_round12), 0, own0, *near_round0, *far_round0)
    moved0 = to_previous_section(dq0)
    back0 = reduce_x(*away0)
    dq1, stay1, *away1 = run(1, info, SPLIT[0], *gathered12)
    moved1 = to_previous_section(dq1)
    back1 = reduce_x(*away1)
    dq2, stay2, *away2 = run(2, after(info, moved0, *back0), SPLIT[0], *gathered12)
    back2 = reduce_x(*away2)
    moved2 = to_previous_section(dq2)
    sums0, sums1 = [
        wide_sum(after(stay, stay2), *back) for stay, back in ((stay0, back0), (stay1, back1))
    ]
    down01 = send(joined(sums0[1], sums1[1]), down)
    sums2 = wide_sum(stay2, *back2)
    down2 = send(sums2[1], down)
    home = joined(sums0[0], sums1[0], sums2[0])
    pair = to_previous_section(wide_sum(home, joined(down01, down2)))
    return (jnp.concatenate([moved0, moved1, moved2], axis=1)[None], pair[0:1], pair[1:2])


def solution(mesh):
    placed = (
        P("section", "ctx", None),
        P("section", "ctx", None),
        P("section", "ctx", None),
        P("section", "ctx", None),
        P("section", None),
        P("section", None, None),
        P("section", None),
    )
    return jax.shard_map(
        per_device,
        mesh=mesh,
        in_specs=placed,
        out_specs=(P("section", "ctx", None), P("section", "ctx", None), P("section", "ctx", None)),
        check_vma=False,
    )
```

```python
import functools
import math

import jax
import jax.numpy as jnp
from jax import lax
from jax.experimental import pallas as pl
from jax.experimental.pallas import tpu as pltpu
from jax.sharding import PartitionSpec as P

HEADS = 64
KV_HEADS = 8
HEAD_DIM = 128
BLK = 128
NBLK = 8
RATIO = HEADS // KV_HEADS
LANES = RATIO * BLK
HALF = 2 * BLK
RING = 4
SPLIT = (3, 3, 2)
SCALE = 1.0 / math.sqrt(HEAD_DIM)
LOG2E = math.log2(math.e)
LOWEST = -3.0e38


def ctx_route(move):
    route = []
    for place in range(NBLK):
        target = move(place // RING, place % RING)
        if target is not None:
            route.append((place, target[0] * RING + target[1] % RING))
    return route


def right(y, x):
    return (y, x + 1)


def left(y, x):
    return (y, x - 1)


def across(y, x):
    return (y, x + 2)


def up(y, x):
    return (1, x) if y == 0 else None


def down(y, x):
    return (0, x) if y == 1 else None


def send(block, move):
    return lax.ppermute(block, "ctx", ctx_route(move))


def to_previous_section(block):
    sections = lax.axis_size("section")
    return lax.ppermute(block, "section", [((s + 1) % sections, s) for s in range(sections)])


def nt_dot(a, b):
    return lax.dot_general(a, b, (((1,), (1,)), ((), ())), preferred_element_type=jnp.float32)


def grads_kernel(by_block, info, ends_ref, q_ref, g_ref, own_ref, left_ref, right_ref, y_ref, x2_ref, ylr_ref,
                 dq_ref, *refs):
    part_refs, (keys, values, bias, weights, wgrads, tops, dq_acc, pair_acc) = refs[:-8], refs[-8:]
    count = info[0]
    row_place = info[9]
    y = row_place // RING
    x = lax.rem(row_place, RING)
    other = 1 - y
    pairs = lax.div(count + 1, 2)

    def place_of(row, column):
        return row * RING + lax.rem(column + RING, RING)

    @pl.when(pl.program_id(0) == 0)
    def _():
        row = row_place * BLK + lax.broadcasted_iota(jnp.int32, (BLK, BLK), 1)
        inner = lax.broadcasted_iota(jnp.int32, (BLK, BLK), 0)
        for entry in range(NBLK):
            block = info[1 + entry]
            column = block * BLK + inner
            ends = jnp.broadcast_to(ends_ref[pl.ds(block, 1), :], (BLK, BLK)).T
            good = (column <= row) & (row < ends) & (entry < count)
            bias[pl.ds(entry * BLK, BLK), :] = jnp.where(good, 0.0, -jnp.inf)

    slots = (
        (own_ref, (), place_of(y, x)),
        (left_ref, (), place_of(y, x - 1)),
        (right_ref, (), place_of(y, x + 1)),
        (y_ref, (), place_of(other, x)),
        (x2_ref, (0,), place_of(y, x + 2)),
        (x2_ref, (1,), place_of(other, x + 2)),
        (ylr_ref, (0,), place_of(other, x - 1)),
        (ylr_ref, (1,), place_of(other, x + 1)),
    )
    for ref, lead, place in slots:
        rows = pl.ds(pl.multiple_of(place * BLK, BLK), BLK)
        keys[rows, :] = ref[(*lead, 0)]
        values[rows, :] = ref[(*lead, 1)]

    pair_acc[...] = jnp.zeros_like(pair_acc)
    dq_acc[...] = jnp.zeros_like(dq_acc)

    def block_rows(entry):
        return pl.ds(pl.multiple_of(info[1 + entry] * BLK, BLK), BLK)

    def both(ref, pair):
        return jnp.concatenate([ref[block_rows(2 * pair), :], ref[block_rows(2 * pair + 1), :]], axis=0)

    def two_heads(ref, part):
        first = part * HALF
        return jnp.concatenate([ref[0, :, first:first + BLK], ref[0, :, first + BLK:first + HALF]], axis=0)

    def first_pass(pair, carry):
        top, total, delta = carry
        key_pair = both(keys, pair)
        value_pair = both(values, pair)
        rows = pl.ds(pl.multiple_of(pair * HALF, HALF), HALF)
        mask = bias[rows, :]
        mask2 = jnp.concatenate([mask, mask], axis=1)
        new_top, new_total, new_delta = [], [], []
        for part in range(RATIO // 2):
            lanes = slice(part * HALF, (part + 1) * HALF)
            scores = nt_dot(key_pair, two_heads(q_ref, part)) + mask2
            wgrad = nt_dot(value_pair, two_heads(g_ref, part))
            old = top[:, lanes]
            now = jnp.maximum(old, jnp.max(scores, axis=0, keepdims=True))
            weight = jnp.exp2((scores - now) * (SCALE * LOG2E))
            shrink = jnp.exp2((old - now) * (SCALE * LOG2E))
            weights[rows, lanes] = weight
            wgrads[rows, lanes] = wgrad
            new_top.append(now)
            new_total.append(total[:, lanes] * shrink + jnp.sum(weight, axis=0, keepdims=True))
            new_delta.append(delta[:, lanes] * shrink + jnp.sum(weight * wgrad, axis=0, keepdims=True))
        top = jnp.concatenate(new_top, axis=1)
        tops[pl.ds(pair, 1), :] = top
        return (top, jnp.concatenate(new_total, axis=1), jnp.concatenate(new_delta, axis=1))

    zero = jnp.zeros((1, LANES), jnp.float32)
    top, total, delta = lax.fori_loop(0, pairs, first_pass, (jnp.full((1, LANES), LOWEST, jnp.float32), zero, zero))
    inverse = 1.0 / total
    delta = delta * inverse

    def second_pass(pair, carry):
        key_pair_t = both(keys, pair).T
        rows = pl.ds(pl.multiple_of(pair * HALF, HALF), HALF)
        factor = jnp.exp2((tops[pl.ds(pair, 1), :] - top) * (SCALE * LOG2E)) * inverse
        key_sum = jnp.zeros((HALF, HEAD_DIM), jnp.float32)
        value_sum = jnp.zeros((HALF, HEAD_DIM), jnp.float32)
        for part in range(RATIO // 2):
            lanes = slice(part * HALF, (part + 1) * HALF)
            attention = weights[rows, lanes] * factor[:, lanes]
            score_grad = (attention * ((wgrads[rows, lanes] - delta[:, lanes]) * SCALE)).astype(jnp.bfloat16)
            value_sum += jnp.dot(attention.astype(jnp.bfloat16), two_heads(g_ref, part), preferred_element_type=jnp.float32)
            key_sum += jnp.dot(score_grad, two_heads(q_ref, part), preferred_element_type=jnp.float32)
            dq_acc[:, lanes] += jnp.dot(key_pair_t, score_grad, preferred_element_type=jnp.float32)

        pair_acc[0, block_rows(2 * pair), :] = key_sum[:BLK]
        pair_acc[1, block_rows(2 * pair), :] = value_sum[:BLK]

        @pl.when(2 * pair + 1 < count)
        def _():
            pair_acc[0, block_rows(2 * pair + 1), :] = key_sum[BLK:]
            pair_acc[1, block_rows(2 * pair + 1), :] = value_sum[BLK:]

        return carry

    lax.fori_loop(0, pairs, second_pass, 0)
    for head in range(RATIO):
        lanes = slice(head * BLK, (head + 1) * BLK)
        dq_ref[:, lanes] = dq_acc[:, lanes].T.astype(jnp.bfloat16)
    if by_block:
        outs = [(part_refs[0], (block,), block) for block in range(NBLK)]
    else:
        stay_ref, to_left_ref, to_right_ref, far_ref = part_refs
        leads = [(stay_ref, 0), (to_left_ref, 0), (to_right_ref, 0), (stay_ref, 1)]
        leads += [(far_ref, 0), (far_ref, 1), (to_left_ref, 1), (to_right_ref, 1)]
        outs = [(ref, (at,), slot[2]) for (ref, at), slot in zip(leads, slots)]
    for ref, lead, place in outs:
        rows = pl.ds(pl.multiple_of(place * BLK, BLK), BLK)
        for which in range(2):
            ref[(*lead, which)] = pair_acc[which, rows, :].astype(ref.dtype)


def chunk_grads(by_block, at, base, groups, info, ends, queries, out_grad, own, from_left, from_right, from_y, from_x2, from_ylr):
    width = LANES
    wide = pl.BlockSpec((1, BLK, width), lambda g, *_: (0, 0, base + at + g))
    one = pl.BlockSpec((2, BLK, HEAD_DIM), lambda g, *_: (0, 0, base + at + g))
    two = pl.BlockSpec((2, 2, BLK, HEAD_DIM), lambda g, *_: (0, 0, 0, at + g))
    outs = (NBLK,) if by_block else (2, 2, 2, 2)
    columns = groups * HEAD_DIM
    return pl.pallas_call(
        functools.partial(grads_kernel, by_block),
        grid_spec=pltpu.PrefetchScalarGridSpec(
            num_scalar_prefetch=1,
            grid=(groups,),
            in_specs=[pl.BlockSpec((NBLK, BLK), lambda g, *_: (0, 0)), wide, wide, one, one, one, one, two, two],
            out_specs=[pl.BlockSpec((BLK, width), lambda g, *_: (0, g))]
            + [pl.BlockSpec((n, 2, BLK, HEAD_DIM), lambda g, *_: (0, 0, 0, g)) for n in outs],
            scratch_shapes=[
                pltpu.VMEM((NBLK * BLK, HEAD_DIM), jnp.bfloat16),
                pltpu.VMEM((NBLK * BLK, HEAD_DIM), jnp.bfloat16),
                pltpu.VMEM((NBLK * BLK, BLK), jnp.float32),
                pltpu.VMEM((NBLK * BLK, LANES), jnp.float32),
                pltpu.VMEM((NBLK * BLK, LANES), jnp.float32),
                pltpu.VMEM((NBLK, LANES), jnp.float32),
                pltpu.VMEM((HEAD_DIM, LANES), jnp.float32),
                pltpu.VMEM((2, NBLK * BLK, HEAD_DIM), jnp.float32),
            ],
        ),
        out_shape=[
            jax.ShapeDtypeStruct((BLK, groups * width), jnp.bfloat16),
        ]
        + [jax.ShapeDtypeStruct((n, 2, BLK, columns), jnp.bfloat16) for n in outs],
        compiler_params=pltpu.CompilerParams(vmem_limit_bytes=40 * 1024 * 1024),
        cost_estimate=pl.CostEstimate(
            flops=groups * RATIO * NBLK * 50 * BLK ** 3, bytes_accessed=groups * 6 * BLK * width, transcendentals=0
        ),
    )(info, ends, queries, out_grad, own, from_left, from_right, from_y, from_x2, from_ylr)


def wide_sum(*terms):
    return functools.reduce(jnp.add, [term.astype(jnp.float32) for term in terms]).astype(jnp.bfloat16)


def after(value, *others):
    return lax.optimization_barrier((value, *others))[0]


def per_device(queries, key_states, value_states, out_grad, node_end, block_list, block_count):
    place = lax.axis_index("ctx")
    info = jnp.concatenate([block_count[0, place][None], block_list[0, place], place[None].astype(jnp.int32)])
    ends = node_end.reshape(NBLK, BLK)
    firsts = [sum(SPLIT[:chunk]) for chunk in range(4)]

    def mine(first, end):
        span = slice(firsts[first] * HEAD_DIM, firsts[end] * HEAD_DIM)
        return jnp.concatenate([key_states[:, :, span], value_states[:, :, span]])

    def near_round(own):
        from_y = send(own, up)
        return send(own, right), send(own, left), from_y

    def far_round(own, near):
        sides = send(jnp.stack([near[0], near[1]]), up)
        return send(jnp.stack([own, near[2]]), across), sides

    def joined(*parts):
        return jnp.concatenate(parts, axis=2)

    def reduce_x(to_left, to_right, far):
        return send(to_left, left), send(to_right, right), send(far, across)

    def run(chunk, held, base, *gathered):
        return chunk_grads(
            False, firsts[chunk] - base, base, SPLIT[chunk], held, ends, queries, out_grad, *gathered
        )

    own = mine(0, 3)
    near = near_round(own)
    cut = SPLIT[0] * HEAD_DIM
    far_round0 = far_round(own[:, :, :cut], [part[:, :, :cut] for part in near])
    rest = (own[:, :, cut:], [part[:, :, cut:] for part in near])
    far_round12 = far_round(*rest)
    gathered12 = (own, *near, *far_round12)

    dq0, stay0, *away0 = run(0, info, 0, own, *near, *far_round0)
    moved0 = to_previous_section(dq0)
    back0 = reduce_x(*away0)
    dq1, stay1, *away1 = run(1, info, SPLIT[0], *gathered12)
    moved1 = to_previous_section(dq1)
    back1 = reduce_x(*away1)
    dq2, stay2, *away2 = run(2, after(info, moved0, *back0), SPLIT[0], *gathered12)
    back2 = reduce_x(*away2)
    moved2 = to_previous_section(dq2)
    sums0, sums1 = [
        wide_sum(after(stay, stay2), *back) for stay, back in ((stay0, back0), (stay1, back1))
    ]
    down01 = send(joined(sums0[1], sums1[1]), down)
    sums2 = wide_sum(stay2, *back2)
    down2 = send(sums2[1], down)
    home = joined(sums0[0], sums1[0], sums2[0])
    pair = to_previous_section(wide_sum(home, joined(down01, down2)))
    return (jnp.concatenate([moved0, moved1, moved2], axis=1)[None], pair[0:1], pair[1:2])


def solution(mesh):
    placed = (
        P("section", "ctx", None),
        P("section", "ctx", None),
        P("section", "ctx", None),
        P("section", "ctx", None),
        P("section", None),
        P("section", None, None),
        P("section", None),
    )
    return jax.shard_map(
        per_device,
        mesh=mesh,
        in_specs=placed,
        out_specs=(P("section", "ctx", None), P("section", "ctx", None), P("section", "ctx", None)),
        check_vma=False,
    )
```

```python
import functools
import math

import jax
import jax.numpy as jnp
from jax import lax
from jax.experimental import pallas as pl
from jax.experimental.pallas import tpu as pltpu
from jax.sharding import PartitionSpec as P

HEADS = 64
KV_HEADS = 8
HEAD_DIM = 128
BLK = 128
NBLK = 8
RATIO = HEADS // KV_HEADS
LANES = RATIO * BLK
HALF = 2 * BLK
RING = 4
SPLIT = (3, 3, 2)
SCALE = 1.0 / math.sqrt(HEAD_DIM)
LOG2E = math.log2(math.e)
LOWEST = -3.0e38


def ctx_route(move):
    route = []
    for place in range(NBLK):
        target = move(place // RING, place % RING)
        if target is not None:
            route.append((place, target[0] * RING + target[1] % RING))
    return route


def right(y, x):
    return (y, x + 1)


def left(y, x):
    return (y, x - 1)


def across(y, x):
    return (y, x + 2)


def up(y, x):
    return (1, x) if y == 0 else None


def down(y, x):
    return (0, x) if y == 1 else None


def send(block, move):
    return lax.ppermute(block, "ctx", ctx_route(move))


def to_previous_section(block):
    sections = lax.axis_size("section")
    return lax.ppermute(block, "section", [((s + 1) % sections, s) for s in range(sections)])


def nt_dot(a, b):
    return lax.dot_general(a, b, (((1,), (1,)), ((), ())), preferred_element_type=jnp.float32)


def grads_kernel(by_block, info, ends_ref, q_ref, g_ref, own_ref, left_ref, right_ref, y_ref, x2_ref, ylr_ref,
                 dq_ref, *refs):
    part_refs, (keys, values, bias, weights, wgrads, tops, dq_acc, pair_acc) = refs[:-8], refs[-8:]
    count = info[0]
    row_place = info[9]
    y = row_place // RING
    x = lax.rem(row_place, RING)
    other = 1 - y
    pairs = lax.div(count + 1, 2)

    def place_of(row, column):
        return row * RING + lax.rem(column + RING, RING)

    @pl.when(pl.program_id(0) == 0)
    def _():
        row = row_place * BLK + lax.broadcasted_iota(jnp.int32, (BLK, BLK), 1)
        inner = lax.broadcasted_iota(jnp.int32, (BLK, BLK), 0)
        for entry in range(NBLK):
            block = info[1 + entry]
            column = block * BLK + inner
            ends = jnp.broadcast_to(ends_ref[pl.ds(block, 1), :], (BLK, BLK)).T
            good = (column <= row) & (row < ends) & (entry < count)
            bias[pl.ds(entry * BLK, BLK), :] = jnp.where(good, 0.0, -jnp.inf)

    slots = (
        (own_ref, (), place_of(y, x)),
        (left_ref, (), place_of(y, x - 1)),
        (right_ref, (), place_of(y, x + 1)),
        (y_ref, (), place_of(other, x)),
        (x2_ref, (0,), place_of(y, x + 2)),
        (x2_ref, (1,), place_of(other, x + 2)),
        (ylr_ref, (0,), place_of(other, x - 1)),
        (ylr_ref, (1,), place_of(other, x + 1)),
    )
    for ref, lead, place in slots:
        rows = pl.ds(pl.multiple_of(place * BLK, BLK), BLK)
        keys[rows, :] = ref[(*lead, 0)]
        values[rows, :] = ref[(*lead, 1)]

    pair_acc[...] = jnp.zeros_like(pair_acc)
    dq_acc[...] = jnp.zeros_like(dq_acc)

    def block_rows(entry):
        return pl.ds(pl.multiple_of(info[1 + entry] * BLK, BLK), BLK)

    def both(ref, pair):
        return jnp.concatenate([ref[block_rows(2 * pair), :], ref[block_rows(2 * pair + 1), :]], axis=0)

    def two_heads(ref, part):
        first = part * HALF
        return jnp.concatenate([ref[0, :, first:first + BLK], ref[0, :, first + BLK:first + HALF]], axis=0)

    def first_pass(pair, carry):
        top, total, delta = carry
        key_pair = both(keys, pair)
        value_pair = both(values, pair)
        rows = pl.ds(pl.multiple_of(pair * HALF, HALF), HALF)
        mask = bias[rows, :]
        mask2 = jnp.concatenate([mask, mask], axis=1)
        new_top, new_total, new_delta = [], [], []
        for part in range(RATIO // 2):
            lanes = slice(part * HALF, (part + 1) * HALF)
            scores = nt_dot(key_pair, two_heads(q_ref, part)) + mask2
            wgrad = nt_dot(value_pair, two_heads(g_ref, part))
            old = top[:, lanes]
            now = jnp.maximum(old, jnp.max(scores, axis=0, keepdims=True))
            weight = jnp.exp2((scores - now) * (SCALE * LOG2E))
            shrink = jnp.exp2((old - now) * (SCALE * LOG2E))
            weights[rows, lanes] = weight
            wgrads[rows, lanes] = wgrad
            new_top.append(now)
            new_total.append(total[:, lanes] * shrink + jnp.sum(weight, axis=0, keepdims=True))
            new_delta.append(delta[:, lanes] * shrink + jnp.sum(weight * wgrad, axis=0, keepdims=True))
        top = jnp.concatenate(new_top, axis=1)
        tops[pl.ds(pair, 1), :] = top
        return (top, jnp.concatenate(new_total, axis=1), jnp.concatenate(new_delta, axis=1))

    zero = jnp.zeros((1, LANES), jnp.float32)
    top, total, delta = lax.fori_loop(0, pairs, first_pass, (jnp.full((1, LANES), LOWEST, jnp.float32), zero, zero))
    inverse = 1.0 / total
    delta = delta * inverse

    def second_pass(pair, carry):
        key_pair_t = both(keys, pair).T
        rows = pl.ds(pl.multiple_of(pair * HALF, HALF), HALF)
        factor = jnp.exp2((tops[pl.ds(pair, 1), :] - top) * (SCALE * LOG2E)) * inverse
        key_sum = jnp.zeros((HALF, HEAD_DIM), jnp.float32)
        value_sum = jnp.zeros((HALF, HEAD_DIM), jnp.float32)
        for part in range(RATIO // 2):
            lanes = slice(part * HALF, (part + 1) * HALF)
            attention = weights[rows, lanes] * factor[:, lanes]
            score_grad = (attention * ((wgrads[rows, lanes] - delta[:, lanes]) * SCALE)).astype(jnp.bfloat16)
            value_sum += jnp.dot(attention.astype(jnp.bfloat16), two_heads(g_ref, part), preferred_element_type=jnp.float32)
            key_sum += jnp.dot(score_grad, two_heads(q_ref, part), preferred_element_type=jnp.float32)
            dq_acc[:, lanes] += jnp.dot(key_pair_t, score_grad, preferred_element_type=jnp.float32)

        pair_acc[0, block_rows(2 * pair), :] = key_sum[:BLK].astype(pair_acc.dtype)
        pair_acc[1, block_rows(2 * pair), :] = value_sum[:BLK].astype(pair_acc.dtype)

        @pl.when(2 * pair + 1 < count)
        def _():
            pair_acc[0, block_rows(2 * pair + 1), :] = key_sum[BLK:].astype(pair_acc.dtype)
            pair_acc[1, block_rows(2 * pair + 1), :] = value_sum[BLK:].astype(pair_acc.dtype)

        return carry

    lax.fori_loop(0, pairs, second_pass, 0)
    for head in range(RATIO):
        lanes = slice(head * BLK, (head + 1) * BLK)
        dq_ref[:, lanes] = dq_acc[:, lanes].T.astype(jnp.bfloat16)
    if by_block:
        outs = [(part_refs[0], (block,), block) for block in range(NBLK)]
    else:
        stay_ref, to_left_ref, to_right_ref, far_ref = part_refs
        leads = [(stay_ref, 0), (to_left_ref, 0), (to_right_ref, 0), (stay_ref, 1)]
        leads += [(far_ref, 0), (far_ref, 1), (to_left_ref, 1), (to_right_ref, 1)]
        outs = [(ref, (at,), slot[2]) for (ref, at), slot in zip(leads, slots)]
    for ref, lead, place in outs:
        rows = pl.ds(pl.multiple_of(place * BLK, BLK), BLK)
        for which in range(2):
            ref[(*lead, which)] = pair_acc[which, rows, :].astype(ref.dtype)


def chunk_grads(by_block, at, base, groups, info, ends, queries, out_grad, own, from_left, from_right, from_y, from_x2, from_ylr):
    width = LANES
    wide = pl.BlockSpec((1, BLK, width), lambda g, *_: (0, 0, base + at + g))
    one = pl.BlockSpec((2, BLK, HEAD_DIM), lambda g, *_: (0, 0, base + at + g))
    two = pl.BlockSpec((2, 2, BLK, HEAD_DIM), lambda g, *_: (0, 0, 0, at + g))
    outs = (NBLK,) if by_block else (2, 2, 2, 2)
    columns = groups * HEAD_DIM
    return pl.pallas_call(
        functools.partial(grads_kernel, by_block),
        grid_spec=pltpu.PrefetchScalarGridSpec(
            num_scalar_prefetch=1,
            grid=(groups,),
            in_specs=[pl.BlockSpec((NBLK, BLK), lambda g, *_: (0, 0)), wide, wide, one, one, one, one, two, two],
            out_specs=[pl.BlockSpec((BLK, width), lambda g, *_: (0, g))]
            + [pl.BlockSpec((n, 2, BLK, HEAD_DIM), lambda g, *_: (0, 0, 0, g)) for n in outs],
            scratch_shapes=[
                pltpu.VMEM((NBLK * BLK, HEAD_DIM), jnp.bfloat16),
                pltpu.VMEM((NBLK * BLK, HEAD_DIM), jnp.bfloat16),
                pltpu.VMEM((NBLK * BLK, BLK), jnp.float32),
                pltpu.VMEM((NBLK * BLK, LANES), jnp.float32),
                pltpu.VMEM((NBLK * BLK, LANES), jnp.float32),
                pltpu.VMEM((NBLK, LANES), jnp.float32),
                pltpu.VMEM((HEAD_DIM, LANES), jnp.float32),
                pltpu.VMEM((2, NBLK * BLK, HEAD_DIM), jnp.bfloat16),
            ],
        ),
        out_shape=[
            jax.ShapeDtypeStruct((BLK, groups * width), jnp.bfloat16),
        ]
        + [jax.ShapeDtypeStruct((n, 2, BLK, columns), jnp.bfloat16) for n in outs],
        compiler_params=pltpu.CompilerParams(vmem_limit_bytes=40 * 1024 * 1024),
        cost_estimate=pl.CostEstimate(
            flops=groups * RATIO * NBLK * 50 * BLK ** 3, bytes_accessed=groups * 6 * BLK * width, transcendentals=0
        ),
    )(info, ends, queries, out_grad, own, from_left, from_right, from_y, from_x2, from_ylr)


def wide_sum(*terms):
    return functools.reduce(jnp.add, [term.astype(jnp.float32) for term in terms]).astype(jnp.bfloat16)


def after(value, *others):
    return lax.optimization_barrier((value, *others))[0]


def per_device(queries, key_states, value_states, out_grad, node_end, block_list, block_count):
    place = lax.axis_index("ctx")
    info = jnp.concatenate([block_count[0, place][None], block_list[0, place], place[None].astype(jnp.int32)])
    ends = node_end.reshape(NBLK, BLK)
    firsts = [sum(SPLIT[:chunk]) for chunk in range(4)]

    def mine(first, end):
        span = slice(firsts[first] * HEAD_DIM, firsts[end] * HEAD_DIM)
        return jnp.concatenate([key_states[:, :, span], value_states[:, :, span]])

    def near_round(own):
        from_y = send(own, up)
        return send(own, right), send(own, left), from_y

    def far_round(own, near):
        sides = send(jnp.stack([near[0], near[1]]), up)
        return send(jnp.stack([own, near[2]]), across), sides

    def joined(*parts):
        return jnp.concatenate(parts, axis=2)

    def reduce_x(to_left, to_right, far):
        return send(to_left, left), send(to_right, right), send(far, across)

    def run(chunk, held, base, *gathered):
        return chunk_grads(
            False, firsts[chunk] - base, base, SPLIT[chunk], held, ends, queries, out_grad, *gathered
        )

    own = mine(0, 3)
    near = near_round(own)
    cut = SPLIT[0] * HEAD_DIM
    far_round0 = far_round(own[:, :, :cut], [part[:, :, :cut] for part in near])
    rest = (own[:, :, cut:], [part[:, :, cut:] for part in near])
    far_round12 = far_round(*rest)
    gathered12 = (own, *near, *far_round12)

    dq0, stay0, *away0 = run(0, info, 0, own, *near, *far_round0)
    moved0 = to_previous_section(dq0)
    back0 = reduce_x(*away0)
    dq1, stay1, *away1 = run(1, info, SPLIT[0], *gathered12)
    moved1 = to_previous_section(dq1)
    back1 = reduce_x(*away1)
    dq2, stay2, *away2 = run(2, after(info, moved0, *back0), SPLIT[0], *gathered12)
    back2 = reduce_x(*away2)
    moved2 = to_previous_section(dq2)
    sums0, sums1 = [
        wide_sum(after(stay, stay2), *back) for stay, back in ((stay0, back0), (stay1, back1))
    ]
    down01 = send(joined(sums0[1], sums1[1]), down)
    sums2 = wide_sum(stay2, *back2)
    down2 = send(sums2[1], down)
    home = joined(sums0[0], sums1[0], sums2[0])
    pair = to_previous_section(wide_sum(home, joined(down01, down2)))
    return (jnp.concatenate([moved0, moved1, moved2], axis=1)[None], pair[0:1], pair[1:2])


def solution(mesh):
    placed = (
        P("section", "ctx", None),
        P("section", "ctx", None),
        P("section", "ctx", None),
        P("section", "ctx", None),
        P("section", None),
        P("section", None, None),
        P("section", None),
    )
    return jax.shard_map(
        per_device,
        mesh=mesh,
        in_specs=placed,
        out_specs=(P("section", "ctx", None), P("section", "ctx", None), P("section", "ctx", None)),
        check_vma=False,
    )
```
